32 devices in a mesh: grp: 2 (over x), doc: 16 (over z, y, core).
Axes of the slice: x: 2, y: 2, z: 4, core: 2. Of those that a mesh axis runs over, the one named last changes fastest.
Arguments:
- queries: bfloat16 [128, 2, 4096], P('doc'), may hold values from -6 to 6
- documents: bfloat16 [16384, 2, 4096], P(('grp', 'doc')), parts along dimension 0, may hold values from -450 to 450
- eigvals: float32 [2, 64, 64], replicated, may hold values from 0.01 to 1
- basis_in: float32 [2, 64, 64], replicated, may hold values from -1 to 1, as said below
- basis_out: float32 [2, 64, 64], replicated, may hold values from -1 to 1, as said below
Outputs:
- standardized: float32 [16384, 128], P(('grp', 'doc')), parts along dimension 0
The draws below stay inside these ranges and needn't reach their ends.
There are 2 independent parts, one for each index of `grp`. The reference program is written for one: setup_inputs(seed, part) draws one part's arguments, and reference() takes and returns one part's arrays. A program takes and returns all parts, laid end to end along the dimension named above; an argument that names none is the same for every part. Nothing has to cross between parts.
Inputs may be any that keep to these rules, and one draw needn't show every extreme that they name: `basis_in`: each layer's matrix is orthogonal. `basis_out`: each layer's matrix is orthogonal.
All inputs are finite; a program needn't handle non-finite values.
Results may differ from the reference program's by a relative error of at most 0.003.
Values may be sent and summed in bfloat16 or wider, within the bound.
A program may use at most 128 MiB of HBM per device.

```python
import math
import jax
import jax.numpy as jnp
from jax import lax

DOUT = 64
DIN = 64
LAYERS = 2
PROJ = 4096
DOCS = 8192
QUERIES = 128


def reflections(key, width):
    first = jax.random.normal(jax.random.fold_in(key, 1), (LAYERS, width), jnp.float32)
    second = jax.random.normal(jax.random.fold_in(key, 2), (LAYERS, width), jnp.float32)
    first = first / jnp.sqrt(jnp.sum(first * first, axis=-1, keepdims=True))
    second = second / jnp.sqrt(jnp.sum(second * second, axis=-1, keepdims=True))
    inner = jnp.sum(first * second, axis=-1)[:, None, None]
    ident = jnp.eye(width, dtype=jnp.float32)[None]
    return ident - 2.0 * first[:, :, None] * first[:, None, :] - 2.0 * second[:, :, None] * second[:, None, :] + 4.0 * inner * first[:, :, None] * second[:, None, :]


def draw_basis_in(key, part):
    key = jax.random.fold_in(key, 3)
    return reflections(key, DIN)


def draw_basis_out(key, part):
    key = jax.random.fold_in(key, 5)
    return reflections(key, DOUT)


def draw_documents(key, part):
    key = jax.random.fold_in(key, 7)
    positions = jnp.arange(DOCS, dtype=jnp.float32)
    trend = 1.0 + 2.0 * positions / max(DOCS - 1, 1)
    common = jnp.clip(jax.random.normal(jax.random.fold_in(key, 11), (LAYERS, DOUT * DIN), jnp.float32), -4.0, 4.0)
    weight = 0.6
    top = 10.0
    noise = jnp.clip(jax.random.normal(jax.random.fold_in(key, 17), (DOCS, LAYERS, DOUT * DIN), jnp.float32), -4.0, 4.0)
    scale = jnp.exp(jax.random.uniform(jax.random.fold_in(key, 13), (DOCS,), jnp.float32, 0.0, math.log(top))) * trend
    return (scale[:, None, None] * (weight * common[None] + noise)).astype(jnp.bfloat16)


def levels(rng, dims, cuts, least, largest):
    factor_of = 1.0
    for axis_at, shards_of in cuts:
        draws = jax.random.uniform(jax.random.fold_in(jax.random.fold_in(rng, 6), axis_at), (shards_of,), jnp.float32, least / len(cuts), largest / len(cuts))
        factor_of = factor_of * jnp.repeat(jnp.exp(draws), dims[axis_at] // shards_of).reshape((-1,) + (1,) * (len(dims) - 1 - axis_at))
    return factor_of


def bell_draw(key, extent, deviation, most, shards=(), kind=jnp.bfloat16):
    gain = levels(key, extent, shards, -0.22, 0.18) if shards else 1.0
    values = jax.random.normal(key, extent, jnp.float32) * deviation * gain
    return jnp.minimum(jnp.maximum(values, -most), most).astype(kind)


def setup_inputs(seed: int = 0, part: int = 0) -> dict:
    seeds = jax.random.split(jax.random.key(seed), 6)
    part_keys = jax.random.split(jax.random.fold_in(seeds[5], part), 6)
    queries = bell_draw(seeds[0], (QUERIES, LAYERS, PROJ), 1.0, 6.0, ((0, 16),))
    documents = draw_documents(jax.random.fold_in(jax.random.fold_in(seeds[5], part), 71), part)
    eigvals = jnp.clip(jnp.exp(jax.random.uniform(seeds[2], (LAYERS, DOUT, DIN), jnp.float32, math.log(0.01), math.log(1.0))), 0.01, 1.0)
    basis_in = draw_basis_in(jax.random.fold_in(seeds[5], 71), part)
    basis_out = draw_basis_out(jax.random.fold_in(seeds[5], 71), part)
    return {"queries": queries, "documents": documents, "eigvals": eigvals, "basis_in": basis_in, "basis_out": basis_out}


damp_scale = 0.1
eps_var = 1e-06

def precondition(queries, eigvals, basis_in, basis_out):
    count = queries.shape[0]
    grads = queries.astype(jnp.float32).reshape(count, LAYERS, DOUT, DIN)
    damping = damp_scale * lax.optimization_barrier(jnp.mean(eigvals, axis=(1, 2), keepdims=True))
    rotated = jnp.einsum('lai,qlab,lbj->qlij', basis_out, grads, basis_in, precision=lax.Precision.HIGHEST)
    scaled = rotated / (eigvals + damping)[None]
    back = jnp.einsum('lia,qlab,ljb->qlij', basis_out, scaled, basis_in, precision=lax.Precision.HIGHEST)
    return back.reshape(count, LAYERS * DOUT * DIN).astype(jnp.bfloat16)

def reference(queries, documents, eigvals, basis_in, basis_out):
    prepared = precondition(queries, eigvals, basis_in, basis_out)
    flat_docs = documents.reshape(documents.shape[0], LAYERS * DOUT * DIN)
    scores = jnp.dot(flat_docs, prepared.T, preferred_element_type=jnp.float32)
    mean = lax.optimization_barrier(jnp.mean(scores, axis=0))
    centered = scores - mean
    var = lax.optimization_barrier(jnp.mean(centered * centered, axis=0))
    return centered * lax.rsqrt(var + eps_var)
```

```python
import functools

import jax
import jax.numpy as jnp
from jax import lax
from jax.experimental import pallas as pl
from jax.experimental.pallas import tpu as pltpu
from jax.sharding import PartitionSpec as P

SIDE = 64
damp_scale = 0.1
eps_var = 1e-06
F32 = jnp.float32
BF16 = jnp.bfloat16
MESH = pl.DeviceIdType.MESH
CHUNKS = 2
DOC_COPIES = 8


def flip(value, bits):
    at = 1
    while at <= bits:
        if bits & at:
            value = value + at - 2 * at * ((value // at) % 2)
        at *= 2
    return value


def split(x):
    hi = x.astype(BF16)
    return hi, (x - hi.astype(F32)).astype(BF16)


def dot3(a, b, dims):
    ah, al = a
    bh, bl = b
    dot = functools.partial(
        lax.dot_general, dimension_numbers=(dims, ((), ())), preferred_element_type=F32
    )
    total = dot(ah, bh) + dot(ah, bl)
    if al is not None:
        total = total + dot(al, bh)
    return total


def precondition(core, query_ref, eig_ref, in_ref, out_ref, wide, rows, put):
    lane = lax.broadcasted_iota(jnp.int32, (8, 128), 1)
    low = lane < SIDE
    for pair in range(SIDE // 2):
        wide[pair] = query_ref[:, pl.ds(pair * 128, 128)].astype(F32)
        first = wide[pair, pl.ds(0, 8, stride=2), :]
        second = wide[pair, pl.ds(1, 8, stride=2), :]
        rows[pl.ds(pair * 16, 8), :] = jnp.where(low, first, pltpu.roll(second, SIDE, 1))
        rows[pl.ds(pair * 16 + 8, 8), :] = jnp.where(low, pltpu.roll(first, SIDE, 1), second)

    zero = jnp.zeros((SIDE, SIDE), F32)
    diag = split(
        jnp.concatenate(
            [
                jnp.concatenate([in_ref[0], zero], axis=1),
                jnp.concatenate([zero, in_ref[1]], axis=1),
            ],
            axis=0,
        )
    )
    back_out = jnp.concatenate([out_ref[0], out_ref[1]], axis=0)
    fwd_out = split(jnp.concatenate([out_ref[0].T, out_ref[1].T], axis=0))
    back_out = split(back_out)
    inverse = []
    for layer in range(2):
        eig = eig_ref[layer]
        damping = damp_scale * (jnp.sum(eig) / (SIDE * SIDE))
        inverse.append(1.0 / (eig + damping))
    inverse = jnp.concatenate(inverse, axis=1)

    rows[...] = dot3((rows[...].astype(BF16), None), diag, ((1,), (0,)))
    by_a = jnp.concatenate([rows[pl.ds(q, SIDE, stride=8), :] for q in range(8)], axis=1)
    own = lax.broadcasted_iota(jnp.int32, (SIDE, 128), 1) < SIDE
    own = jnp.concatenate([own.astype(F32)] * 8, axis=1) > 0.5
    both = dot3(fwd_out, split(by_a), ((1,), (0,)))
    scaled = jnp.where(own, both[:SIDE], both[SIDE:]) * jnp.concatenate([inverse] * 8, axis=1)
    both = dot3(back_out, split(scaled), ((1,), (0,)))
    back = jnp.where(own, both[:SIDE], both[SIDE:])
    for q in range(8):
        rows[pl.ds(q, SIDE, stride=8), :] = back[:, q * 128 : (q + 1) * 128]
    rows[...] = dot3(split(rows[...]), diag, ((1,), (1,)))

    swap = core == 1
    for pair in range(SIDE // 2):
        even = rows[pl.ds(pair * 16, 8), :]
        odd = rows[pl.ds(pair * 16 + 8, 8), :]
        one = jnp.where(low, even, pltpu.roll(odd, SIDE, 1))
        two = jnp.where(low, pltpu.roll(even, SIDE, 1), odd)
        upper = jnp.where(swap, two, one)
        lower = jnp.where(swap, one, two)
        put(pair, jnp.concatenate([upper, lower], axis=0).astype(BF16))


def kernel(
    n, query_ref, docs_ref, eig_ref, in_ref, out_basis_ref, result_ref,
    docs, gathered, acc, score, wide, rows, stats,
    doc_sem, send_sem, recv_sem, stat_send, stat_recv,
):
    depth = n // 4
    grp = lax.axis_index("grp")
    me = lax.axis_index("doc")
    other = flip(grp, 1)
    z, y, core = me // 4, (me // 2) % 2, me % 2
    leads = core == grp % 2
    beside, sibling = flip(me, 2), flip(me, 1)

    doc_rows = docs.shape[0]
    part = doc_rows // DOC_COPIES
    flat = docs_ref.reshape(doc_rows, docs.shape[1])
    loads = [
        pltpu.make_async_copy(
            flat.at[pl.ds(i * part, part), :], docs.at[pl.ds(i * part, part), :], doc_sem.at[i]
        )
        for i in range(DOC_COPIES)
    ]

    barrier = pltpu.get_barrier_semaphore()
    for k in range(1, n):
        pl.semaphore_signal(
            barrier, inc=1, device_id=(grp, lax.rem(me + k, n)), device_id_type=MESH
        )
    pl.semaphore_signal(barrier, inc=1, device_id=(other, me), device_id_type=MESH)
    for load in loads:
        load.start()

    def slot(plane, row, c):
        return c * (n // 2) + plane * 2 + row

    mine = slot(z, y, core)

    def put(pair, block):
        gathered[mine, :, pl.ds(pair * 128, 128)] = block

    precondition(core, query_ref, eig_ref, in_ref, out_basis_ref, wide, rows, put)
    pl.semaphore_wait(barrier, n)

    width = gathered.shape[2] // CHUNKS
    half = width // 2
    used = [0]
    lead_sends, follow_sends, all_sends = [], [], []

    def copy(where, block, chunk, piece, device):
        start = chunk * width + (half if piece == 1 else 0)
        ref = gathered.at[block, :, pl.ds(start, width if piece is None else half)]
        made = pltpu.make_async_remote_copy(
            src_ref=ref,
            dst_ref=ref,
            send_sem=send_sem.at[used[0]],
            recv_sem=recv_sem.at[block, chunk, 1 if piece == 1 else 0],
            device_id=device,
            device_id_type=MESH,
        )
        used[0] += 1
        made.start()
        where.append(made)

    def arrived(block, chunk, piece):
        start = chunk * width + (half if piece == 1 else 0)
        ref = gathered.at[block, :, pl.ds(start, width if piece is None else half)]
        pltpu.make_async_remote_copy(
            src_ref=ref,
            dst_ref=ref,
            send_sem=send_sem.at[0],
            recv_sem=recv_sem.at[block, chunk, 1 if piece == 1 else 0],
            device_id=(grp, sibling),
            device_id_type=MESH,
        ).wait_recv()

    to_beside, to_other, to_sibling = (grp, beside), (other, me), (grp, sibling)

    @pl.when(leads)
    def _():
        sends = lead_sends
        for chunk in range(CHUNKS):
            copy(sends, mine, chunk, None, to_beside)
            for step in range(1, depth):
                copy(sends, mine, chunk, None, (grp, flip(z, step) * 4 + me % 4))
            copy(sends, mine, chunk, None, to_sibling)

        def near(step, chunk):
            block = slot(flip(z, step), y, core)
            arrived(block, chunk, None)
            copy(sends, block, chunk, None, to_other)
            copy(sends, block, chunk, None, to_beside)
            copy(sends, block, chunk, None, to_sibling)

        def far(step, chunk):
            block = slot(flip(z, step), 1 - y, core)
            arrived(block, chunk, None)
            copy(sends, block, chunk, 0, to_other)
            copy(sends, block, chunk, None, to_sibling)

        for chunk in range(CHUNKS):
            for step in range(1, depth):
                near(step, chunk)
                far(step - 1, chunk)
            far(depth - 1, chunk)
        for made in sends:
            made.wait_send()

    lead_used, used[0] = used[0], 0

    @pl.when(jnp.logical_not(leads))
    def _():
        sends = follow_sends
        for chunk in range(CHUNKS):
            copy(sends, mine, chunk, 1, to_beside)
            copy(sends, mine, chunk, None, to_sibling)

        def near(step, chunk):
            block = slot(flip(z, step), y, core)
            arrived(block, chunk, None)
            copy(sends, block, chunk, 1, to_beside)
            copy(sends, block, chunk, None, to_sibling)

        def far(step, chunk):
            block = slot(flip(z, step), 1 - y, core)
            for piece in (1, 0):
                arrived(block, chunk, piece)
            copy(sends, block, chunk, None, to_sibling)

        for chunk in range(CHUNKS):
            for step in range(1, depth):
                near(step, chunk)
                far(step - 1, chunk)
            far(depth - 1, chunk)
        for made in sends:
            made.wait_send()

    for chunk in range(CHUNKS):
        for step in range(depth):
            arrived(slot(flip(z, step), y, 1 - core), chunk, None)
            arrived(slot(flip(z, step), 1 - y, 1 - core), chunk, None)
    for load in loads:
        load.wait()

    lanes = n * 8
    for chunk in range(CHUNKS):
        cols = pl.ds(chunk * width, width)
        right = gathered[:, :, cols].reshape(n * 16, width)
        product = lax.dot_general(
            docs[:, cols], right, (((1,), (1,)), ((), ())), preferred_element_type=F32
        )
        for tile in range(n // 8):
            piece = product[:, tile * 128 : (tile + 1) * 128]
            acc[tile] = piece if chunk == 0 else acc[tile] + piece

    count = doc_rows // 2
    for at in range(0, lanes, 128):
        upper = lax.broadcasted_iota(jnp.int32, (count, 128), 1) // 8 % 2 == 0
        even, odd = pl.ds(0, count, stride=2), pl.ds(1, count, stride=2)
        first, second = at // 128, (lanes + at) // 128
        direct = jnp.where(upper, acc[first, even, :], acc[second, even, :])
        cross = jnp.where(upper, acc[second, odd, :], acc[first, odd, :])
        cross = jnp.where(upper, pltpu.roll(cross, 120, 1), pltpu.roll(cross, 8, 1))
        score[:, pl.ds(at, 128)] = direct + cross

    values = score[...]
    local_mean = jnp.sum(values, axis=0, keepdims=True) / count
    away = values - local_mean
    spread = jnp.sum(away * away, axis=0, keepdims=True)
    row = lax.broadcasted_iota(jnp.int32, (8, lanes), 0)
    stats[me] = jnp.where(row == 0, local_mean, spread)
    shares = []
    for k in range(1, n):
        share = pltpu.make_async_remote_copy(
            src_ref=stats.at[me],
            dst_ref=stats.at[me],
            send_sem=stat_send.at[k],
            recv_sem=stat_recv.at[k],
            device_id=(grp, lax.rem(me + k, n)),
            device_id_type=MESH,
        )
        share.start()
        shares.append(share)
    for k in range(1, n):
        source = lax.rem(me + n - k, n)
        pltpu.make_async_remote_copy(
            src_ref=stats.at[me],
            dst_ref=stats.at[source],
            send_sem=stat_send.at[k],
            recv_sem=stat_recv.at[k],
            device_id=(grp, source),
            device_id_type=MESH,
        ).wait_recv()
    for share in shares:
        share.wait_send()
    merged = stats[...]
    means, spreads = merged[:, 0:1, :], merged[:, 1:2, :]
    mean = jnp.sum(means, axis=0) / n
    shift = means - mean[None]
    var = (jnp.sum(spreads, axis=0) + count * jnp.sum(shift * shift, axis=0)) / (count * n)
    result_ref[...] = (values - mean) * lax.rsqrt(var + eps_var)


def shards(queries, documents, eigvals, basis_in, basis_out):
    n = lax.axis_size("doc")
    doc_rows, layers, proj = documents.shape
    vmem = pl.BlockSpec(memory_space=pltpu.VMEM)
    queries = queries.reshape(queries.shape[0] * layers, proj)
    most = CHUNKS * (6 * (n // 4) + 4)
    return pl.pallas_call(
        functools.partial(kernel, n),
        out_shape=jax.ShapeDtypeStruct((doc_rows, n * 8), F32),
        in_specs=[vmem, pl.BlockSpec(memory_space=pl.ANY), vmem, vmem, vmem],
        out_specs=vmem,
        scratch_shapes=[
            pltpu.VMEM((doc_rows * layers, proj), BF16),
            pltpu.VMEM((n, 16, proj), BF16),
            pltpu.VMEM((n // 8, doc_rows * layers, 128), F32),
            pltpu.VMEM((doc_rows, n * 8), F32),
            pltpu.VMEM((proj // 128, 16, 128), F32),
            pltpu.VMEM((8 * SIDE, 128), F32),
            pltpu.VMEM((n, 8, n * 8), F32),
            pltpu.SemaphoreType.DMA((DOC_COPIES,)),
            pltpu.SemaphoreType.DMA((most,)),
            pltpu.SemaphoreType.DMA((n, CHUNKS, 2)),
            pltpu.SemaphoreType.DMA((n,)),
            pltpu.SemaphoreType.DMA((n,)),
        ],
        compiler_params=pltpu.CompilerParams(
            collective_id=0, has_side_effects=True, vmem_limit_bytes=56 * 1024 * 1024
        ),
        cost_estimate=pl.CostEstimate(
            flops=2 * doc_rows * layers * proj * n * 16,
            bytes_accessed=2 * doc_rows * layers * proj,
            transcendentals=0,
        ),
    )(queries, documents, eigvals, basis_in, basis_out)


def solution(mesh):
    placed = (P("doc", None, None), P(("grp", "doc"), None, None), P(), P(), P())
    return jax.shard_map(
        shards, mesh=mesh, in_specs=placed, out_specs=P(("grp", "doc"), None), check_vma=False
    )
```

```python
import functools

import jax
import jax.numpy as jnp
from jax import lax
from jax.experimental import pallas as pl
from jax.experimental.pallas import tpu as pltpu
from jax.sharding import PartitionSpec as P

SIDE = 64
damp_scale = 0.1
eps_var = 1e-06
F32 = jnp.float32
BF16 = jnp.bfloat16
MESH = pl.DeviceIdType.MESH
CHUNKS = 2
LAG = 1
DOC_COPIES = 8


def flip(value, bits):
    at = 1
    while at <= bits:
        if bits & at:
            value = value + at - 2 * at * ((value // at) % 2)
        at *= 2
    return value


def split(x):
    hi = x.astype(BF16)
    return hi, (x - hi.astype(F32)).astype(BF16)


def dot3(a, b, dims):
    ah, al = a
    bh, bl = b
    dot = functools.partial(
        lax.dot_general, dimension_numbers=(dims, ((), ())), preferred_element_type=F32
    )
    total = dot(ah, bh) + dot(ah, bl)
    if al is not None:
        total = total + dot(al, bh)
    return total


def precondition(core, query_ref, eig_ref, in_ref, out_ref, wide, rows, put):
    lane = lax.broadcasted_iota(jnp.int32, (8, 128), 1)
    low = lane < SIDE
    for pair in range(SIDE // 2):
        wide[pair] = query_ref[:, pl.ds(pair * 128, 128)].astype(F32)
        first = wide[pair, pl.ds(0, 8, stride=2), :]
        second = wide[pair, pl.ds(1, 8, stride=2), :]
        rows[pl.ds(pair * 16, 8), :] = jnp.where(low, first, pltpu.roll(second, SIDE, 1))
        rows[pl.ds(pair * 16 + 8, 8), :] = jnp.where(low, pltpu.roll(first, SIDE, 1), second)

    zero = jnp.zeros((SIDE, SIDE), F32)
    diag = split(
        jnp.concatenate(
            [
                jnp.concatenate([in_ref[0], zero], axis=1),
                jnp.concatenate([zero, in_ref[1]], axis=1),
            ],
            axis=0,
        )
    )
    back_out = jnp.concatenate([out_ref[0], out_ref[1]], axis=0)
    fwd_out = split(jnp.concatenate([out_ref[0].T, out_ref[1].T], axis=0))
    back_out = split(back_out)
    inverse = []
    for layer in range(2):
        eig = eig_ref[layer]
        damping = damp_scale * (jnp.sum(eig) / (SIDE * SIDE))
        inverse.append(1.0 / (eig + damping))
    inverse = jnp.concatenate(inverse, axis=1)

    rows[...] = dot3((rows[...].astype(BF16), None), diag, ((1,), (0,)))
    by_a = jnp.concatenate([rows[pl.ds(q, SIDE, stride=8), :] for q in range(8)], axis=1)
    own = lax.broadcasted_iota(jnp.int32, (SIDE, 128), 1) < SIDE
    own = jnp.concatenate([own.astype(F32)] * 8, axis=1) > 0.5
    both = dot3(fwd_out, split(by_a), ((1,), (0,)))
    scaled = jnp.where(own, both[:SIDE], both[SIDE:]) * jnp.concatenate([inverse] * 8, axis=1)
    both = dot3(back_out, split(scaled), ((1,), (0,)))
    back = jnp.where(own, both[:SIDE], both[SIDE:])
    for q in range(8):
        rows[pl.ds(q, SIDE, stride=8), :] = back[:, q * 128 : (q + 1) * 128]
    rows[...] = dot3(split(rows[...]), diag, ((1,), (1,)))

    swap = core == 1
    for pair in range(SIDE // 2):
        even = rows[pl.ds(pair * 16, 8), :]
        odd = rows[pl.ds(pair * 16 + 8, 8), :]
        one = jnp.where(low, even, pltpu.roll(odd, SIDE, 1))
        two = jnp.where(low, pltpu.roll(even, SIDE, 1), odd)
        upper = jnp.where(swap, two, one)
        lower = jnp.where(swap, one, two)
        put(pair, jnp.concatenate([upper, lower], axis=0).astype(BF16))


def kernel(
    n, query_ref, docs_ref, eig_ref, in_ref, out_basis_ref, result_ref,
    query, docs, gathered, acc, score, wide, rows, stats,
    doc_sem, send_sem, recv_sem, stat_send, stat_recv,
):
    depth = n // 4
    grp = lax.axis_index("grp")
    me = lax.axis_index("doc")
    other = flip(grp, 1)
    z, y, core = me // 4, (me // 2) % 2, me % 2
    leads = core == grp % 2
    beside, sibling = flip(me, 2), flip(me, 1)

    doc_rows = docs.shape[0]
    part = doc_rows // DOC_COPIES
    flat = docs_ref.reshape(doc_rows, docs.shape[1])
    loads = [
        pltpu.make_async_copy(
            flat.at[pl.ds(i * part, part), :], docs.at[pl.ds(i * part, part), :], doc_sem.at[i]
        )
        for i in range(DOC_COPIES)
    ]

    fetch = pltpu.make_async_copy(
        query_ref.reshape(16, docs.shape[1]), query, doc_sem.at[DOC_COPIES]
    )
    fetch.start()
    barrier = pltpu.get_barrier_semaphore()
    plane_peers = [(grp, flip(me, bits)) for bits in (1, 2, 3)]
    column_peers = [(grp, lax.rem(me + 4 * k, n)) for k in range(1, depth)]
    for peer in plane_peers + column_peers + [(other, me)]:
        pl.semaphore_signal(barrier, inc=1, device_id=peer, device_id_type=MESH)
    for load in loads:
        load.start()

    def slot(plane, row, c):
        return c * (n // 2) + plane * 2 + row

    mine = slot(z, y, core)

    def put(pair, block):
        gathered[mine, :, pl.ds(pair * 128, 128)] = block

    fetch.wait()
    precondition(core, query, eig_ref, in_ref, out_basis_ref, wide, rows, put)
    pl.semaphore_wait(barrier, depth + 3)

    width = gathered.shape[2] // CHUNKS
    half = width // 2
    pending = []

    def columns(chunk, piece):
        start = chunk * width + (half if piece == 1 else 0)
        return pl.ds(start, width if piece is None else half)

    def guard(condition, body):
        pl.when(condition())(body) if condition else body()

    def copy(block, chunk, piece, device, condition=None):
        ref = gathered.at[block, :, columns(chunk, piece)]
        made = pltpu.make_async_remote_copy(
            src_ref=ref,
            dst_ref=ref,
            send_sem=send_sem.at[len(pending)],
            recv_sem=recv_sem.at[block, chunk, 1 if piece == 1 else 0],
            device_id=device,
            device_id_type=MESH,
        )
        made.start()
        pending.append((piece, condition))

    def wait_for(block, chunk, piece, sends=None):
        ref = gathered.at[block, :, columns(chunk, piece)]
        made = pltpu.make_async_remote_copy(
            src_ref=ref,
            dst_ref=ref,
            send_sem=send_sem.at[sends or 0],
            recv_sem=recv_sem.at[block, chunk, 1 if piece == 1 else 0],
            device_id=(grp, sibling),
            device_id_type=MESH,
        )
        made.wait_recv() if sends is None else made.wait_send()

    def drain():
        for at, (piece, condition) in enumerate(pending):
            guard(condition, functools.partial(wait_for, mine, 0, piece, at))
        pending.clear()

    to_beside, to_other, to_sibling = (grp, beside), (other, me), (grp, sibling)

    def planes(dist):
        if dist == 0:
            return [
                (z, 1, None, lambda: z + 1 < depth),
                (z, -1, None, lambda: z >= 1),
            ]
        return [
            (z - dist, 1, lambda: z >= dist,
             lambda: jnp.logical_and(z >= dist, z + 1 < depth)),
            (z + dist, -1, lambda: z + dist < depth,
             lambda: jnp.logical_and(z + dist < depth, z >= 1)),
        ]

    def lead_near(dist, chunk):
        for plane, step, there, further in planes(dist):
            block = slot(plane, y, core)

            def onward():
                copy(block, chunk, None, (grp, me + 4 * step), further)

            def spread():
                copy(block, chunk, None, to_beside, there)
                if dist:
                    copy(block, chunk, None, to_other, there)
                copy(block, chunk, None, to_sibling, there)

            if dist:
                guard(there, functools.partial(wait_for, block, chunk, None))
            guard(further, onward)
            if dist or step < 0:
                guard(there, spread)

    def lead_far(dist, chunk):
        for plane, _, there, _ in planes(dist)[: 2 if dist else 1]:
            block = slot(plane, 1 - y, core)

            def spread():
                wait_for(block, chunk, None)
                copy(block, chunk, 0, to_other, there)
                copy(block, chunk, None, to_sibling, there)

            guard(there, spread)

    def follow_near(dist, chunk):
        for plane, _, there, _ in planes(dist)[: 2 if dist else 1]:
            block = slot(plane, y, core)

            def spread():
                if dist:
                    wait_for(block, chunk, None)
                copy(block, chunk, 1, to_beside, there)
                copy(block, chunk, None, to_sibling, there)

            guard(there, spread)

    def follow_far(dist, chunk):
        for plane, _, there, _ in planes(dist)[: 2 if dist else 1]:
            block = slot(plane, 1 - y, core)

            def spread():
                wait_for(block, chunk, 1)
                wait_for(block, chunk, 0)
                copy(block, chunk, None, to_sibling, there)

            guard(there, spread)

    def walk(near, far):
        for dist in range(depth + LAG):
            for chunk in range(CHUNKS):
                if dist < depth:
                    near(dist, chunk)
                if dist >= LAG:
                    far(dist - LAG, chunk)
        drain()

    @pl.when(leads)
    def _():
        walk(lead_near, lead_far)

    @pl.when(jnp.logical_not(leads))
    def _():
        walk(follow_near, follow_far)

    for chunk in range(CHUNKS):
        for step in range(depth):
            wait_for(slot(step, y, 1 - core), chunk, None)
            wait_for(slot(step, 1 - y, 1 - core), chunk, None)
    for load in loads:
        load.wait()

    lanes = n * 8
    for chunk in range(CHUNKS):
        cols = pl.ds(chunk * width, width)
        right = gathered[:, :, cols].reshape(n * 16, width)
        product = lax.dot_general(
            docs[:, cols], right, (((1,), (1,)), ((), ())), preferred_element_type=F32
        )
        for tile in range(n // 8):
            piece = product[:, tile * 128 : (tile + 1) * 128]
            acc[tile] = piece if chunk == 0 else acc[tile] + piece

    count = doc_rows // 2
    for at in range(0, lanes, 128):
        upper = lax.broadcasted_iota(jnp.int32, (count, 128), 1) // 8 % 2 == 0
        even, odd = pl.ds(0, count, stride=2), pl.ds(1, count, stride=2)
        first, second = at // 128, (lanes + at) // 128
        direct = jnp.where(upper, acc[first, even, :], acc[second, even, :])
        cross = jnp.where(upper, acc[second, odd, :], acc[first, odd, :])
        cross = jnp.where(upper, pltpu.roll(cross, 120, 1), pltpu.roll(cross, 8, 1))
        score[:, pl.ds(at, 128)] = direct + cross

    values = score[...]
    local_mean = jnp.sum(values, axis=0, keepdims=True) / count
    away = values - local_mean
    spread = jnp.sum(away * away, axis=0, keepdims=True)
    row = lax.broadcasted_iota(jnp.int32, (8, lanes), 0)

    def merge(members, weight, mean, spread, first):
        stats[first] = jnp.where(row == 0, mean, spread)
        shares = []
        for at, peer in enumerate(members):
            share = pltpu.make_async_remote_copy(
                src_ref=stats.at[first],
                dst_ref=stats.at[first + 1 + at],
                send_sem=stat_send.at[first + at],
                recv_sem=stat_recv.at[first + at],
                device_id=peer,
                device_id_type=MESH,
            )
            share.start()
            shares.append(share)
        for share in shares:
            share.wait()
        total = len(members) + 1
        merged = [stats[first + at] for at in range(total)]
        middle = sum(part[0:1] for part in merged) / total
        wide_spread = sum(part[1:2] for part in merged)
        shift = sum((part[0:1] - middle) * (part[0:1] - middle) for part in merged)
        return middle, wide_spread + weight * shift

    mean, spread = merge(plane_peers, count, local_mean, spread, 0)
    mean, spread = merge(column_peers, count * 4, mean, spread, 4)
    var = spread / (count * n)
    result_ref[...] = (values - mean) * lax.rsqrt(var + eps_var)


def shards(queries, documents, eigvals, basis_in, basis_out):
    n = lax.axis_size("doc")
    doc_rows, layers, proj = documents.shape
    vmem = pl.BlockSpec(memory_space=pltpu.VMEM)
    most = CHUNKS * (12 * (n // 4))
    return pl.pallas_call(
        functools.partial(kernel, n),
        out_shape=jax.ShapeDtypeStruct((doc_rows, n * 8), F32),
        in_specs=[pl.BlockSpec(memory_space=pl.ANY)] * 2 + [vmem] * 3,
        out_specs=vmem,
        scratch_shapes=[
            pltpu.VMEM((16, proj), BF16),
            pltpu.VMEM((doc_rows * layers, proj), BF16),
            pltpu.VMEM((n, 16, proj), BF16),
            pltpu.VMEM((n // 8, doc_rows * layers, 128), F32),
            pltpu.VMEM((doc_rows, n * 8), F32),
            pltpu.VMEM((proj // 128, 16, 128), F32),
            pltpu.VMEM((8 * SIDE, 128), F32),
            pltpu.VMEM((4 + n // 4, 8, n * 8), F32),
            pltpu.SemaphoreType.DMA((DOC_COPIES + 1,)),
            pltpu.SemaphoreType.DMA((most,)),
            pltpu.SemaphoreType.DMA((n, CHUNKS, 2)),
            pltpu.SemaphoreType.DMA((n,)),
            pltpu.SemaphoreType.DMA((n,)),
        ],
        compiler_params=pltpu.CompilerParams(
            collective_id=0, has_side_effects=True, vmem_limit_bytes=56 * 1024 * 1024
        ),
        cost_estimate=pl.CostEstimate(
            flops=2 * doc_rows * layers * proj * n * 16,
            bytes_accessed=2 * doc_rows * layers * proj,
            transcendentals=0,
        ),
    )(queries, documents, eigvals, basis_in, basis_out)


def solution(mesh):
    placed = (P("doc", None, None), P(("grp", "doc"), None, None), P(), P(), P())
    return jax.shard_map(
        shards, mesh=mesh, in_specs=placed, out_specs=P(("grp", "doc"), None), check_vma=False
    )
```

```python
import functools

import jax
import jax.numpy as jnp
from jax import lax
from jax.experimental import pallas as pl
from jax.experimental.pallas import tpu as pltpu
from jax.sharding import PartitionSpec as P

SIDE = 64
damp_scale = 0.1
eps_var = 1e-06
F32 = jnp.float32
BF16 = jnp.bfloat16
MESH = pl.DeviceIdType.MESH
CHUNKS = 2
LAG = 1
DOC_COPIES = 8


def flip(value, bits):
    at = 1
    while at <= bits:
        if bits & at:
            value = value + at - 2 * at * ((value // at) % 2)
        at *= 2
    return value


def split(x):
    hi = x.astype(BF16)
    return hi, (x - hi.astype(F32)).astype(BF16)


def dot3(a, b, dims):
    ah, al = a
    bh, bl = b
    dot = functools.partial(
        lax.dot_general, dimension_numbers=(dims, ((), ())), preferred_element_type=F32
    )
    total = dot(ah, bh) + dot(ah, bl)
    if al is not None:
        total = total + dot(al, bh)
    return total


def precondition(core, query_ref, eig_ref, in_ref, out_ref, wide, rows, put):
    lane = lax.broadcasted_iota(jnp.int32, (8, 128), 1)
    low = lane < SIDE
    for pair in range(SIDE // 2):
        wide[pair] = query_ref[:, pl.ds(pair * 128, 128)].astype(F32)
        first = wide[pair, pl.ds(0, 8, stride=2), :]
        second = wide[pair, pl.ds(1, 8, stride=2), :]
        rows[pl.ds(pair * 16, 8), :] = jnp.where(low, first, pltpu.roll(second, SIDE, 1))
        rows[pl.ds(pair * 16 + 8, 8), :] = jnp.where(low, pltpu.roll(first, SIDE, 1), second)

    zero = jnp.zeros((SIDE, SIDE), F32)
    diag = split(
        jnp.concatenate(
            [
                jnp.concatenate([in_ref[0], zero], axis=1),
                jnp.concatenate([zero, in_ref[1]], axis=1),
            ],
            axis=0,
        )
    )
    back_out = jnp.concatenate([out_ref[0], out_ref[1]], axis=0)
    fwd_out = split(jnp.concatenate([out_ref[0].T, out_ref[1].T], axis=0))
    back_out = split(back_out)
    inverse = []
    for layer in range(2):
        eig = eig_ref[layer]
        damping = damp_scale * (jnp.sum(eig) / (SIDE * SIDE))
        inverse.append(1.0 / (eig + damping))
    inverse = jnp.concatenate(inverse, axis=1)

    rows[...] = dot3((rows[...].astype(BF16), None), diag, ((1,), (0,)))
    by_a = jnp.concatenate([rows[pl.ds(q, SIDE, stride=8), :] for q in range(8)], axis=1)
    own = lax.broadcasted_iota(jnp.int32, (SIDE, 128), 1) < SIDE
    own = jnp.concatenate([own.astype(F32)] * 8, axis=1) > 0.5
    both = dot3(fwd_out, split(by_a), ((1,), (0,)))
    scaled = jnp.where(own, both[:SIDE], both[SIDE:]) * jnp.concatenate([inverse] * 8, axis=1)
    both = dot3(back_out, split(scaled), ((1,), (0,)))
    back = jnp.where(own, both[:SIDE], both[SIDE:])
    for q in range(8):
        rows[pl.ds(q, SIDE, stride=8), :] = back[:, q * 128 : (q + 1) * 128]
    rows[...] = dot3(split(rows[...]), diag, ((1,), (1,)))

    swap = core == 1
    for pair in range(SIDE // 2):
        even = rows[pl.ds(pair * 16, 8), :]
        odd = rows[pl.ds(pair * 16 + 8, 8), :]
        one = jnp.where(low, even, pltpu.roll(odd, SIDE, 1))
        two = jnp.where(low, pltpu.roll(even, SIDE, 1), odd)
        upper = jnp.where(swap, two, one)
        lower = jnp.where(swap, one, two)
        put(pair, jnp.concatenate([upper, lower], axis=0).astype(BF16))


def kernel(
    n, query_ref, docs_ref, eig_ref, in_ref, out_basis_ref, result_ref,
    query, docs, gathered, acc, score, wide, rows, stats,
    doc_sem, send_sem, recv_sem, stat_send, stat_recv,
):
    depth = n // 4
    grp = lax.axis_index("grp")
    me = lax.axis_index("doc")
    other = flip(grp, 1)
    z, y, core = me // 4, (me // 2) % 2, me % 2
    leads = core == grp % 2
    beside, sibling = flip(me, 2), flip(me, 1)

    doc_rows = docs.shape[0]
    part = doc_rows // DOC_COPIES
    flat = docs_ref.reshape(doc_rows, docs.shape[1])
    loads = [
        pltpu.make_async_copy(
            flat.at[pl.ds(i * part, part), :], docs.at[pl.ds(i * part, part), :], doc_sem.at[i]
        )
        for i in range(DOC_COPIES)
    ]

    fetch = pltpu.make_async_copy(
        query_ref.reshape(16, docs.shape[1]), query, doc_sem.at[DOC_COPIES]
    )
    fetch.start()
    barrier = pltpu.get_barrier_semaphore()
    for peer in [(grp, lax.rem(me + k, n)) for k in range(1, n)] + [(other, me)]:
        pl.semaphore_signal(barrier, inc=1, device_id=peer, device_id_type=MESH)
    for load in loads:
        load.start()

    def slot(plane, row, c):
        return c * (n // 2) + plane * 2 + row

    mine = slot(z, y, core)

    def put(pair, block):
        gathered[mine, :, pl.ds(pair * 128, 128)] = block

    fetch.wait()
    precondition(core, query, eig_ref, in_ref, out_basis_ref, wide, rows, put)
    pl.semaphore_wait(barrier, n)

    width = gathered.shape[2] // CHUNKS
    half = width // 2
    pending = []

    def columns(chunk, piece):
        start = chunk * width + (half if piece == 1 else 0)
        return pl.ds(start, width if piece is None else half)

    def guard(condition, body):
        pl.when(condition())(body) if condition else body()

    def copy(block, chunk, piece, device, condition=None):
        ref = gathered.at[block, :, columns(chunk, piece)]
        made = pltpu.make_async_remote_copy(
            src_ref=ref,
            dst_ref=ref,
            send_sem=send_sem.at[len(pending)],
            recv_sem=recv_sem.at[block, chunk, 1 if piece == 1 else 0],
            device_id=device,
            device_id_type=MESH,
        )
        made.start()
        pending.append((piece, condition))

    def wait_for(block, chunk, piece, sends=None):
        ref = gathered.at[block, :, columns(chunk, piece)]
        made = pltpu.make_async_remote_copy(
            src_ref=ref,
            dst_ref=ref,
            send_sem=send_sem.at[sends or 0],
            recv_sem=recv_sem.at[block, chunk, 1 if piece == 1 else 0],
            device_id=(grp, sibling),
            device_id_type=MESH,
        )
        made.wait_recv() if sends is None else made.wait_send()

    def drain():
        for at, (piece, condition) in enumerate(pending):
            guard(condition, functools.partial(wait_for, mine, 0, piece, at))
        pending.clear()

    to_beside, to_other, to_sibling = (grp, beside), (other, me), (grp, sibling)

    def planes(dist):
        below, above = (lambda: z >= dist), (lambda: z + dist < depth)
        if dist == 0:
            return [(z, 1, None, None)]
        return [(z - dist, 1, below, above), (z + dist, -1, above, below)]

    def lead_near(dist, chunk):
        if dist == 0:
            copy(mine, chunk, None, to_beside)
            for hops in range(1, depth):
                for _, step, _, there in planes(hops):
                    target = (grp, me + 4 * step * hops)
                    guard(there, functools.partial(copy, mine, chunk, None, target, there))
            copy(mine, chunk, None, to_sibling)
            return
        for plane, _, there, _ in planes(dist):
            block = slot(plane, y, core)

            def spread():
                wait_for(block, chunk, None)
                copy(block, chunk, None, to_other, there)
                copy(block, chunk, None, to_beside, there)
                copy(block, chunk, None, to_sibling, there)

            guard(there, spread)

    def lead_far(dist, chunk):
        for plane, _, there, _ in planes(dist):
            block = slot(plane, 1 - y, core)

            def spread():
                wait_for(block, chunk, None)
                copy(block, chunk, 0, to_other, there)
                copy(block, chunk, None, to_sibling, there)

            guard(there, spread)

    def follow_near(dist, chunk):
        for plane, _, there, _ in planes(dist):
            block = slot(plane, y, core)

            def spread():
                if dist:
                    wait_for(block, chunk, None)
                copy(block, chunk, 1, to_beside, there)
                copy(block, chunk, None, to_sibling, there)

            guard(there, spread)

    def follow_far(dist, chunk):
        for plane, _, there, _ in planes(dist):
            block = slot(plane, 1 - y, core)

            def spread():
                wait_for(block, chunk, 1)
                wait_for(block, chunk, 0)
                copy(block, chunk, None, to_sibling, there)

            guard(there, spread)

    def walk(near, far):
        for dist in range(depth + LAG):
            for chunk in range(CHUNKS):
                if dist < depth:
                    near(dist, chunk)
                if dist >= LAG:
                    far(dist - LAG, chunk)
        drain()

    @pl.when(leads)
    def _():
        walk(lead_near, lead_far)

    @pl.when(jnp.logical_not(leads))
    def _():
        walk(follow_near, follow_far)

    for chunk in range(CHUNKS):
        for step in range(depth):
            wait_for(slot(step, y, 1 - core), chunk, None)
            wait_for(slot(step, 1 - y, 1 - core), chunk, None)
    for load in loads:
        load.wait()

    lanes = n * 8
    for chunk in range(CHUNKS):
        cols = pl.ds(chunk * width, width)
        right = gathered[:, :, cols].reshape(n * 16, width)
        product = lax.dot_general(
            docs[:, cols], right, (((1,), (1,)), ((), ())), preferred_element_type=F32
        )
        for tile in range(n // 8):
            piece = product[:, tile * 128 : (tile + 1) * 128]
            acc[tile] = piece if chunk == 0 else acc[tile] + piece

    count = doc_rows // 2
    for at in range(0, lanes, 128):
        upper = lax.broadcasted_iota(jnp.int32, (count, 128), 1) // 8 % 2 == 0
        even, odd = pl.ds(0, count, stride=2), pl.ds(1, count, stride=2)
        first, second = at // 128, (lanes + at) // 128
        direct = jnp.where(upper, acc[first, even, :], acc[second, even, :])
        cross = jnp.where(upper, acc[second, odd, :], acc[first, odd, :])
        cross = jnp.where(upper, pltpu.roll(cross, 120, 1), pltpu.roll(cross, 8, 1))
        score[:, pl.ds(at, 128)] = direct + cross

    values = score[...]
    local_mean = jnp.sum(values, axis=0, keepdims=True) / count
    away = values - local_mean
    spread = jnp.sum(away * away, axis=0, keepdims=True)
    row = lax.broadcasted_iota(jnp.int32, (8, lanes), 0)

    stats[me] = jnp.where(row == 0, local_mean, spread)
    shares = []
    for k in range(1, n):
        share = pltpu.make_async_remote_copy(
            src_ref=stats.at[me],
            dst_ref=stats.at[me],
            send_sem=stat_send.at[k],
            recv_sem=stat_recv.at[k],
            device_id=(grp, lax.rem(me + k, n)),
            device_id_type=MESH,
        )
        share.start()
        shares.append(share)
    for k in range(1, n):
        source = lax.rem(me + n - k, n)
        pltpu.make_async_remote_copy(
            src_ref=stats.at[me],
            dst_ref=stats.at[source],
            send_sem=stat_send.at[k],
            recv_sem=stat_recv.at[k],
            device_id=(grp, source),
            device_id_type=MESH,
        ).wait_recv()
    for share in shares:
        share.wait_send()
    merged = stats[...]
    means, spreads = merged[:, 0:1, :], merged[:, 1:2, :]
    mean = jnp.sum(means, axis=0) / n
    shift = means - mean[None]
    var = (jnp.sum(spreads, axis=0) + count * jnp.sum(shift * shift, axis=0)) / (count * n)
    result_ref[...] = (values - mean) * lax.rsqrt(var + eps_var)


def shards(queries, documents, eigvals, basis_in, basis_out):
    n = lax.axis_size("doc")
    doc_rows, layers, proj = documents.shape
    vmem = pl.BlockSpec(memory_space=pltpu.VMEM)
    most = CHUNKS * (12 * (n // 4))
    return pl.pallas_call(
        functools.partial(kernel, n),
        out_shape=jax.ShapeDtypeStruct((doc_rows, n * 8), F32),
        in_specs=[pl.BlockSpec(memory_space=pl.ANY)] * 2 + [vmem] * 3,
        out_specs=vmem,
        scratch_shapes=[
            pltpu.VMEM((16, proj), BF16),
            pltpu.VMEM((doc_rows * layers, proj), BF16),
            pltpu.VMEM((n, 16, proj), BF16),
            pltpu.VMEM((n // 8, doc_rows * layers, 128), F32),
            pltpu.VMEM((doc_rows, n * 8), F32),
            pltpu.VMEM((proj // 128, 16, 128), F32),
            pltpu.VMEM((8 * SIDE, 128), F32),
            pltpu.VMEM((n, 8, n * 8), F32),
            pltpu.SemaphoreType.DMA((DOC_COPIES + 1,)),
            pltpu.SemaphoreType.DMA((most,)),
            pltpu.SemaphoreType.DMA((n, CHUNKS, 2)),
            pltpu.SemaphoreType.DMA((n,)),
            pltpu.SemaphoreType.DMA((n,)),
        ],
        compiler_params=pltpu.CompilerParams(
            collective_id=0, has_side_effects=True, vmem_limit_bytes=56 * 1024 * 1024
        ),
        cost_estimate=pl.CostEstimate(
            flops=2 * doc_rows * layers * proj * n * 16,
            bytes_accessed=2 * doc_rows * layers * proj,
            transcendentals=0,
        ),
    )(queries, documents, eigvals, basis_in, basis_out)


def solution(mesh):
    placed = (P("doc", None, None), P(("grp", "doc"), None, None), P(), P(), P())
    return jax.shard_map(
        shards, mesh=mesh, in_specs=placed, out_specs=P(("grp", "doc"), None), check_vma=False
    )
```
